128 devices in a mesh: row: 8 (over z, core), col: 16 (over x, y).
Axes of the slice: x: 4, y: 4, z: 4, core: 2. Of those that a mesh axis runs over, the one named last changes fastest.
Arguments:
- amplitudes: float32 [4, 1024, 64, 1024], P(None, 'col', 'row'), may hold values from -6 to 6
- cycle_weights: float32 [4, 1024, 1024], P(None, 'col', 'row'), may hold values from -0.09375 to 0.09375
- residual_in: float32 [1024, 64, 1024], P('col', 'row'), may hold values from -6 to 6
Outputs:
- residual_out: float32 [1024, 64, 1024], P('col', 'row')
The draws below stay inside these ranges and needn't reach their ends.
All inputs are finite; a program needn't handle non-finite values.
Results may differ from the reference program's by a relative error of at most 0.0001.
Values sent between devices are 32-bit elements; how exact they have to be, the bound alone decides.
A program may use at most 192 MiB of HBM per device.

```python
import jax
import jax.numpy as jnp
from jax import lax

O = 64
V = 1024
JW = 4


def with_spikes(result, rng, source, target, shards_of, factor):
    owner, partner = [(jnp.arange(result.shape[position]) // (result.shape[position] // shards_of)).reshape([-1 if axis == position else 1 for axis in range(result.ndim)]) for position in (source, target)]
    chosen = jax.random.permutation(rng, shards_of)[partner]
    strong = (owner == chosen) | (owner == (partner + shards_of // 2) % shards_of)
    return jnp.where(strong, factor * result, result)


def block_scale(key, extent, split, least, top_value):
    loudness = 1.0
    for dim, shards_of in split:
        steps = jax.random.uniform(jax.random.fold_in(jax.random.fold_in(key, 6), dim), (shards_of,), jnp.float32, least / len(split), top_value / len(split))
        loudness = loudness * jnp.repeat(jnp.exp(steps), extent[dim] // shards_of).reshape((-1,) + (1,) * (len(extent) - 1 - dim))
    return loudness


def noise(rng, extent, deviation, limit, cuts=(), dtype=jnp.bfloat16):
    level = block_scale(rng, extent, cuts, -0.22, 0.18) if cuts else 1.0
    values = jax.random.normal(rng, extent, jnp.float32) * deviation * level
    return jnp.minimum(jnp.maximum(values, -limit), limit).astype(dtype)


def heavy_noise(stream_key, dims, deviation, limit, shards, heavy, dtype=jnp.bfloat16):
    values = deviation * jax.random.normal(stream_key, dims, jnp.float32)
    if shards:
        values = values * block_scale(stream_key, dims, shards, -0.22, 0.18)
    return jnp.clip(with_spikes(values, jax.random.fold_in(stream_key, 3), *heavy), -limit, limit).astype(dtype)


def setup_inputs(seed: int = 0) -> dict:
    arg_keys = jax.random.split(jax.random.key(seed), 4)
    amplitudes = heavy_noise(arg_keys[0], (JW, V, O, V), 1.0, 6.0, ((1, 16), (2, 8)), (1, 3, 16, 2.0), jnp.float32)
    cycle_weights = noise(arg_keys[1], (JW, V, V), (JW * V) ** -0.5, 0.09375, ((1, 16), (2, 8)), jnp.float32)
    residual_in = noise(arg_keys[2], (V, O, V), 1.0, 6.0, ((0, 16), (1, 8)), jnp.float32)
    return dict(amplitudes=amplitudes, cycle_weights=cycle_weights, residual_in=residual_in)


def reference(amplitudes, cycle_weights, residual_in):
    def add_slab(running, slab_pair):
        amp_slab, weights = slab_pair
        update = jnp.einsum("bia,bc->aic", amp_slab, weights, precision=lax.Precision.HIGHEST)
        return running + update, jnp.zeros((), jnp.float32)

    start = jnp.zeros(residual_in.shape, jnp.float32)
    cycle_sum, unused = lax.scan(add_slab, start, (amplitudes, cycle_weights))
    return residual_in + cycle_sum
```

```python
import jax
import jax.numpy as jnp
from jax import lax
from jax.experimental import pallas as pl
from jax.experimental.pallas import tpu as pltpu
from jax.sharding import PartitionSpec as P

MESH = pl.DeviceIdType.MESH
F32, BF16 = jnp.float32, jnp.bfloat16


def split(v):
    hi = v.astype(BF16)
    return hi, (v - hi.astype(F32)).astype(BF16)


def kernel(
    amp, wts, out,
    stage, turned, arrived, w_all, w_cross, w_hi, w_lo, l_hi, l_lo, part, relay, final,
    load_sem, wl_sem, w_send, w_recv, core_send, core_recv, z_send, z_recv,
    a_send, a_recv, rel_send, rel_recv, dir_send, dir_recv, mer_send, mer_recv, out_sem,
):
    row, col = lax.axis_index("row"), lax.axis_index("col")
    z, k = row // 2, row % 2
    x, y = col // 4, col % 4
    g = x + k * (y - x)
    s = y + k * (x - y)

    def at(gg, ss):
        return (row, (4 - 3 * k) * (gg % 4) + (1 + 3 * k) * (ss % 4))

    def at_z(zz):
        return (2 * (zz % 4) + k, col)

    other = (2 * z + 1 - k, col)

    def remote(src, dst, send, recv, device):
        return pltpu.make_async_remote_copy(
            src_ref=src, dst_ref=dst, send_sem=send, recv_sem=recv, device_id=device, device_id_type=MESH
        )

    barrier = pltpu.get_barrier_semaphore()
    for d in (1, 2, 3):
        pl.semaphore_signal(barrier, 1, device_id=at(g + d, s), device_id_type=MESH)
        pl.semaphore_signal(barrier, 1, device_id=at(g, s + d), device_id_type=MESH)
    for device in (at_z(z + 1), at_z(z + 3), other):
        pl.semaphore_signal(barrier, 1, device_id=device, device_id_type=MESH)

    half0 = ((s + 2) % 4) // 2

    def block_of(q):
        line0 = 2 * ((g + 1 + q) % 4) + (half0 + q // 4) % 2
        m = q // 2
        u = m // 2
        off = (1 - u) * (2 + m) + u * (3 - m)
        line1 = 2 * ((s + off) % 4) + (g // 2 + 1 + q) % 2
        return line0 + k * (line1 - line0)

    def load(q):
        t = block_of(q)
        return pltpu.make_async_copy(
            amp.at[:, :, :, pl.ds(pl.multiple_of(t * 128, 128), 128)], stage.at[q % 2], load_sem.at[q % 2]
        )

    load(0).start()
    load(1).start()
    own_w = pltpu.make_async_copy(wts, w_all.at[row, g], wl_sem.at[0])
    own_wc = pltpu.make_async_copy(wts, w_cross.at[s], wl_sem.at[1])
    own_w.start()
    own_wc.start()

    pl.semaphore_wait(barrier, 9)

    w_line = [remote(wts, w_all.at[row, g], w_send.at[d], w_recv.at[d], at(g + d + 1, s)) for d in range(3)]
    w_cro = [remote(wts, w_cross.at[s], w_send.at[3 + d], w_recv.at[3 + d], at(g, s + d + 1)) for d in range(3)]
    for copy in w_line + w_cro:
        copy.start()

    def slab(o):
        xx, yy = o // 4, o % 4
        gg = xx + k * (yy - xx)
        r = yy + k * (xx - yy)
        return gg, r

    def send_slab(o):
        gg, r = slab(o)
        return remote(turned.at[o], arrived.at[r, g], a_send.at[o], a_recv.at[4 * r + g], at(gg, s))

    @pl.loop(0, 8)
    def _(q):
        load(q).wait()
        t = block_of(q)
        rows = stage.at[q % 2].reshape(2048, 128)
        for i in range(8):
            v = rows[pl.ds(i, 256, stride=8), :].T
            for e in range(2):
                for h in range(2):
                    turned.at[2 * t + e, h][pl.ds(i, 64, stride=8), :] = v[64 * e : 64 * e + 64, 128 * h : 128 * h + 128]

        @pl.when(q < 6)
        def _():
            load(q + 2).start()

        for e in range(2):
            o = 2 * t + e
            gg, r = slab(o)

            @pl.when(gg != g)
            def _():
                send_slab(o).start()

            @pl.when(gg == g)
            def _():
                pltpu.make_async_copy(turned.at[o], arrived.at[r, g], a_recv.at[4 * r + g]).start()

    def z_copy(n, e, up, sem):
        sl = 2 * (n % 4) + e
        return remote(w_all.at[sl], w_all.at[sl], z_send.at[sem], z_recv.at[sem], at_z(z + 1 if up else z + 3))

    def split_w(n):
        n = n % 4

        @pl.loop(0, 4)
        def _(gg):
            for e in range(2):
                hi, lo = split(w_all[2 * n + e, gg].reshape(256, 128))
                at_rows = pl.ds(pl.multiple_of(gg * 256, 256), 256)
                w_hi[n, at_rows, 128 * e : 128 * e + 128] = hi
                w_lo[n, at_rows, 128 * e : 128 * e + 128] = lo

    own_w.wait()
    own_wc.wait()
    for copy in w_line:
        copy.wait()
    z_copy(z, k, True, k).start()
    z_copy(z, k, False, 2 + k).start()
    for copy in w_cro:
        copy.wait()
    swap = remote(w_cross, w_all.at[row], core_send, core_recv, other)
    swap.start()
    swap.wait()
    z_copy(z, 1 - k, True, 1 - k).start()
    z_copy(z, 1 - k, False, 3 - k).start()
    split_w(z)
    z_copy(z, 0, True, 0).wait()
    z_copy(z + 3, 0, True, 4).start()
    z_copy(z, 1, False, 3).wait()
    z_copy(z + 1, 1, False, 5).start()
    z_copy(z, 1, True, 1).wait()
    z_copy(z, 0, False, 2).wait()
    split_w(z + 3)
    split_w(z + 1)
    z_copy(z + 3, 0, True, 4).wait()
    z_copy(z + 1, 1, False, 5).wait()
    split_w(z + 2)

    def a_arrive(r, gg):
        return remote(turned.at[0], arrived.at[r, gg], a_send.at[0], a_recv.at[4 * r + gg], other)

    def multiply(m, r, then):
        r = r % 4
        for gg in range(4):
            a_arrive(r, gg).wait_recv()

        @pl.loop(0, 4)
        def _(gg):
            for h in range(2):
                hi, lo = split(arrived[r, gg, h])
                lanes = pl.ds(pl.multiple_of(256 * gg + 128 * h, 128), 128)
                l_hi[:, lanes] = hi
                l_lo[:, lanes] = lo

        @pl.loop(0, 4)
        def _(n):
            total = jnp.dot(l_hi[...], w_hi[n], preferred_element_type=F32)
            total += jnp.dot(l_hi[...], w_lo[n], preferred_element_type=F32)
            total += jnp.dot(l_lo[...], w_hi[n], preferred_element_type=F32)
            part[m, n] = total.reshape(64, 8, 256)
            if then is not None:
                then(n)

    low, high = pl.ds(0, 32), pl.ds(32, 32)

    def relay_up(n):
        return remote(part.at[0, n, low], relay.at[0, n], rel_send.at[0, n], rel_recv.at[0, n], at(g, s + 1))

    def relay_down(n):
        return remote(part.at[0, n, high], relay.at[1, n], rel_send.at[1, n], rel_recv.at[1, n], at(g, s + 3))

    def direct_up(n):
        return remote(part.at[1, n, high], final.at[0, n, high], dir_send.at[0, n], dir_recv.at[0, n], at(g, s + 1))

    def direct_down(n):
        return remote(part.at[2, n, low], final.at[1, n, low], dir_send.at[1, n], dir_recv.at[1, n], at(g, s + 3))

    def merged_up(n):
        return remote(part.at[1, n, low], final.at[0, n, low], mer_send.at[0, n], mer_recv.at[0, n], at(g, s + 1))

    def merged_down(n):
        return remote(part.at[2, n, high], final.at[1, n, high], mer_send.at[1, n], mer_recv.at[1, n], at(g, s + 3))

    def send_relays(n):
        relay_up(n).start()
        relay_down(n).start()

    multiply(0, s + 2, send_relays)
    multiply(1, s + 1, lambda n: direct_up(n).start())
    multiply(2, s + 3, lambda n: direct_down(n).start())
    multiply(3, s, None)

    @pl.loop(0, 4)
    def _(n):
        relay_up(n).wait()
        part[1, n, low] += relay[0, n]
        merged_up(n).start()
        relay_down(n).wait()
        part[2, n, high] += relay[1, n]
        merged_down(n).start()

    def put(n):
        return pltpu.make_async_copy(
            part.at[3, n], out.at[:, :, pl.ds(pl.multiple_of(n * 256, 256), 256)], out_sem.at[n]
        )

    @pl.loop(0, 4)
    def _(n):
        direct_up(n).wait()
        direct_down(n).wait()
        merged_up(n).wait()
        merged_down(n).wait()
        part[3, n] += final[0, n] + final[1, n]
        put(n).start()

    for n in range(4):
        put(n).wait()

    @pl.loop(0, 16)
    def _(o):
        gg, r = slab(o)

        @pl.when(gg != g)
        def _():
            send_slab(o).wait_send()


def shards(amplitudes, cycle_weights, residual_in):
    dma = pltpu.SemaphoreType.DMA
    cycle_sum = pl.pallas_call(
        kernel,
        out_shape=jax.ShapeDtypeStruct((64, 8, 1024), F32),
        in_specs=[pl.BlockSpec(memory_space=pl.ANY)] * 2,
        out_specs=pl.BlockSpec(memory_space=pl.ANY),
        scratch_shapes=[
            pltpu.VMEM((2, 4, 64, 8, 128), F32),
            pltpu.VMEM((16, 2, 512, 128), F32),
            pltpu.VMEM((4, 4, 2, 512, 128), F32),
            pltpu.VMEM((8, 4, 4, 64, 128), F32),
            pltpu.VMEM((4, 4, 64, 128), F32),
            pltpu.VMEM((4, 1024, 256), BF16),
            pltpu.VMEM((4, 1024, 256), BF16),
            pltpu.VMEM((512, 1024), BF16),
            pltpu.VMEM((512, 1024), BF16),
            pltpu.VMEM((4, 4, 64, 8, 256), F32),
            pltpu.VMEM((2, 4, 32, 8, 256), F32),
            pltpu.VMEM((2, 4, 64, 8, 256), F32),
            dma((2,)), dma((2,)), dma((6,)), dma((6,)), dma, dma, dma((6,)), dma((6,)),
            dma((16,)), dma((16,)), dma((2, 4)), dma((2, 4)), dma((2, 4)), dma((2, 4)), dma((2, 4)), dma((2, 4)), dma((4,)),
        ],
        compiler_params=pltpu.CompilerParams(collective_id=0, has_side_effects=True, vmem_limit_bytes=60 << 20),
        cost_estimate=pl.CostEstimate(flops=2 * 3 * 512 * 4096 * 1024, bytes_accessed=12 << 20, transcendentals=0),
        name="cycle_sum",
    )(amplitudes, cycle_weights)
    return residual_in + cycle_sum


def solution(mesh):
    return jax.shard_map(
        shards,
        mesh=mesh,
        in_specs=(P(None, "col", "row", None), P(None, "col", "row"), P("col", "row", None)),
        out_specs=P("col", "row", None),
        check_vma=False,
    )
```

```python
import jax
import jax.numpy as jnp
from jax import lax
from jax.experimental import pallas as pl
from jax.experimental.pallas import tpu as pltpu
from jax.sharding import PartitionSpec as P

MESH = pl.DeviceIdType.MESH
F32, BF16 = jnp.float32, jnp.bfloat16


def split(v):
    hi = v.astype(BF16)
    return hi, (v - hi.astype(F32)).astype(BF16)


def kernel(
    amp, wts, res, out,
    stage, turned, arrived, w_all, w_cross, w_hi, w_lo, l_hi, l_lo, part, relay, final,
    load_sem, wl_sem, w_send, w_recv, core_send, core_recv, z_send, z_recv,
    a_send, a_recv, rel_send, rel_recv, dir_send, dir_recv, mer_send, mer_recv, res_sem,
):
    row, col = lax.axis_index("row"), lax.axis_index("col")
    z, k = row // 2, row % 2
    x, y = col // 4, col % 4
    g = x + k * (y - x)
    s = y + k * (x - y)

    def at(gg, ss):
        return (row, (4 - 3 * k) * (gg % 4) + (1 + 3 * k) * (ss % 4))

    def at_z(zz):
        return (2 * (zz % 4) + k, col)

    other = (2 * z + 1 - k, col)

    def remote(src, dst, send, recv, device):
        return pltpu.make_async_remote_copy(
            src_ref=src, dst_ref=dst, send_sem=send, recv_sem=recv, device_id=device, device_id_type=MESH
        )

    barrier = pltpu.get_barrier_semaphore()
    for d in (1, 2, 3):
        pl.semaphore_signal(barrier, 1, device_id=at(g + d, s), device_id_type=MESH)
        pl.semaphore_signal(barrier, 1, device_id=at(g, s + d), device_id_type=MESH)
    for device in (at_z(z + 1), at_z(z + 3), other):
        pl.semaphore_signal(barrier, 1, device_id=device, device_id_type=MESH)

    half0 = ((s + 2) % 4) // 2

    def block_of(q):
        line0 = 2 * ((g + 1 + q) % 4) + (half0 + q // 4) % 2
        m = q // 2
        u = m // 2
        off = (1 - u) * (2 + m) + u * (3 - m)
        line1 = 2 * ((s + off) % 4) + (g // 2 + 1 + q) % 2
        return line0 + k * (line1 - line0)

    def load(q):
        t = block_of(q)
        return pltpu.make_async_copy(
            amp.at[:, :, :, pl.ds(pl.multiple_of(t * 128, 128), 128)], stage.at[q % 2], load_sem.at[q % 2]
        )

    load(0).start()
    load(1).start()
    own_w = pltpu.make_async_copy(wts, w_all.at[row, g], wl_sem.at[0])
    own_wc = pltpu.make_async_copy(wts, w_cross.at[s], wl_sem.at[1])
    residual = pltpu.make_async_copy(res, out, res_sem)
    own_w.start()
    own_wc.start()

    residual.start()

    pl.semaphore_wait(barrier, 9)

    w_line = [remote(wts, w_all.at[row, g], w_send.at[d], w_recv.at[d], at(g + d + 1, s)) for d in range(3)]
    w_cro = [remote(wts, w_cross.at[s], w_send.at[3 + d], w_recv.at[3 + d], at(g, s + d + 1)) for d in range(3)]
    for copy in w_line + w_cro:
        copy.start()

    def slab(o):
        xx, yy = o // 4, o % 4
        gg = xx + k * (yy - xx)
        r = yy + k * (xx - yy)
        return gg, r

    def send_slab(o):
        gg, r = slab(o)
        return remote(turned.at[o], arrived.at[r, g], a_send.at[o], a_recv.at[4 * r + g], at(gg, s))

    @pl.loop(0, 8)
    def _(q):
        load(q).wait()
        t = block_of(q)
        rows = stage.at[q % 2].reshape(2048, 128)
        for i in range(8):
            v = rows[pl.ds(i, 256, stride=8), :].T
            for e in range(2):
                for h in range(2):
                    turned.at[2 * t + e, h][pl.ds(i, 64, stride=8), :] = v[64 * e : 64 * e + 64, 128 * h : 128 * h + 128]

        @pl.when(q < 6)
        def _():
            load(q + 2).start()

        for e in range(2):
            o = 2 * t + e
            gg, r = slab(o)

            @pl.when(gg != g)
            def _():
                send_slab(o).start()

            @pl.when(gg == g)
            def _():
                pltpu.make_async_copy(turned.at[o], arrived.at[r, g], a_recv.at[4 * r + g]).start()

    def z_copy(n, e, up, sem):
        sl = 2 * (n % 4) + e
        return remote(w_all.at[sl], w_all.at[sl], z_send.at[sem], z_recv.at[sem], at_z(z + 1 if up else z + 3))

    def split_w(n):
        n = n % 4

        @pl.loop(0, 4)
        def _(gg):
            for e in range(2):
                hi, lo = split(w_all[2 * n + e, gg].reshape(256, 128))
                at_rows = pl.ds(pl.multiple_of(gg * 256, 256), 256)
                w_hi[n, at_rows, 128 * e : 128 * e + 128] = hi
                w_lo[n, at_rows, 128 * e : 128 * e + 128] = lo

    own_w.wait()
    own_wc.wait()
    for copy in w_line:
        copy.wait()
    z_copy(z, k, True, k).start()
    z_copy(z, k, False, 2 + k).start()
    for copy in w_cro:
        copy.wait()
    swap = remote(w_cross, w_all.at[row], core_send, core_recv, other)
    swap.start()
    swap.wait()
    z_copy(z, 1 - k, True, 1 - k).start()
    z_copy(z, 1 - k, False, 3 - k).start()
    split_w(z)
    z_copy(z, 0, True, 0).wait()
    z_copy(z + 3, 0, True, 4).start()
    z_copy(z, 1, False, 3).wait()
    z_copy(z + 1, 1, False, 5).start()
    z_copy(z, 1, True, 1).wait()
    z_copy(z, 0, False, 2).wait()
    split_w(z + 3)
    split_w(z + 1)
    z_copy(z + 3, 0, True, 4).wait()
    z_copy(z + 1, 1, False, 5).wait()
    split_w(z + 2)

    def a_arrive(r, gg):
        return remote(turned.at[0], arrived.at[r, gg], a_send.at[0], a_recv.at[4 * r + gg], other)

    def multiply(m, r, then):
        r = r % 4
        for gg in range(4):
            a_arrive(r, gg).wait_recv()

        @pl.loop(0, 4)
        def _(gg):
            for h in range(2):
                hi, lo = split(arrived[r, gg, h])
                lanes = pl.ds(pl.multiple_of(256 * gg + 128 * h, 128), 128)
                l_hi[:, lanes] = hi
                l_lo[:, lanes] = lo

        @pl.loop(0, 4)
        def _(n):
            total = jnp.dot(l_hi[...], w_hi[n], preferred_element_type=F32)
            total += jnp.dot(l_hi[...], w_lo[n], preferred_element_type=F32)
            total += jnp.dot(l_lo[...], w_hi[n], preferred_element_type=F32)
            part[m, n] = total.reshape(64, 8, 256)
            if then is not None:
                then(n)

    low, high = pl.ds(0, 32), pl.ds(32, 32)

    def relay_up(n):
        return remote(part.at[0, n, low], relay.at[0, n], rel_send.at[0, n], rel_recv.at[0, n], at(g, s + 1))

    def relay_down(n):
        return remote(part.at[0, n, high], relay.at[1, n], rel_send.at[1, n], rel_recv.at[1, n], at(g, s + 3))

    def direct_up(n):
        return remote(part.at[1, n, high], final.at[0, n, high], dir_send.at[0, n], dir_recv.at[0, n], at(g, s + 1))

    def direct_down(n):
        return remote(part.at[2, n, low], final.at[1, n, low], dir_send.at[1, n], dir_recv.at[1, n], at(g, s + 3))

    def merged_up(n):
        return remote(part.at[1, n, low], final.at[0, n, low], mer_send.at[0, n], mer_recv.at[0, n], at(g, s + 1))

    def merged_down(n):
        return remote(part.at[2, n, high], final.at[1, n, high], mer_send.at[1, n], mer_recv.at[1, n], at(g, s + 3))

    def send_relays(n):
        relay_up(n).start()
        relay_down(n).start()

    multiply(0, s + 2, send_relays)
    multiply(1, s + 1, lambda n: direct_up(n).start())
    multiply(2, s + 3, lambda n: direct_down(n).start())
    multiply(3, s, None)

    @pl.loop(0, 4)
    def _(n):
        relay_up(n).wait()
        part[1, n, low] += relay[0, n]
        merged_up(n).start()
        relay_down(n).wait()
        part[2, n, high] += relay[1, n]
        merged_down(n).start()

    residual.wait()

    @pl.loop(0, 4)
    def _(n):
        direct_up(n).wait()
        direct_down(n).wait()
        merged_up(n).wait()
        merged_down(n).wait()
        out[:, :, pl.ds(pl.multiple_of(n * 256, 256), 256)] += part[3, n] + final[0, n] + final[1, n]

    @pl.loop(0, 16)
    def _(o):
        gg, r = slab(o)

        @pl.when(gg != g)
        def _():
            send_slab(o).wait_send()


def shards(amplitudes, cycle_weights, residual_in):
    dma = pltpu.SemaphoreType.DMA
    return pl.pallas_call(
        kernel,
        out_shape=pltpu.VMEM((64, 8, 1024), F32),
        in_specs=[pl.BlockSpec(memory_space=pl.ANY)] * 3,
        out_specs=pl.BlockSpec(memory_space=pltpu.VMEM),
        scratch_shapes=[
            pltpu.VMEM((2, 4, 64, 8, 128), F32),
            pltpu.VMEM((16, 2, 512, 128), F32),
            pltpu.VMEM((4, 4, 2, 512, 128), F32),
            pltpu.VMEM((8, 4, 4, 64, 128), F32),
            pltpu.VMEM((4, 4, 64, 128), F32),
            pltpu.VMEM((4, 1024, 256), BF16),
            pltpu.VMEM((4, 1024, 256), BF16),
            pltpu.VMEM((512, 1024), BF16),
            pltpu.VMEM((512, 1024), BF16),
            pltpu.VMEM((4, 4, 64, 8, 256), F32),
            pltpu.VMEM((2, 4, 32, 8, 256), F32),
            pltpu.VMEM((2, 4, 64, 8, 256), F32),
            dma((2,)), dma((2,)), dma((6,)), dma((6,)), dma, dma, dma((6,)), dma((6,)),
            dma((16,)), dma((16,)), dma((2, 4)), dma((2, 4)), dma((2, 4)), dma((2, 4)), dma((2, 4)), dma((2, 4)), dma,
        ],
        compiler_params=pltpu.CompilerParams(collective_id=0, has_side_effects=True, vmem_limit_bytes=54 << 20),
        cost_estimate=pl.CostEstimate(flops=2 * 3 * 512 * 4096 * 1024, bytes_accessed=12 << 20, transcendentals=0),
        name="cycle_sum",
    )(amplitudes, cycle_weights, residual_in)


def solution(mesh):
    return jax.shard_map(
        shards,
        mesh=mesh,
        in_specs=(P(None, "col", "row", None), P(None, "col", "row"), P("col", "row", None)),
        out_specs=P("col", "row", None),
        check_vma=False,
    )
```

```python
import jax
import jax.numpy as jnp
from jax import lax
from jax.experimental import pallas as pl
from jax.experimental.pallas import tpu as pltpu
from jax.sharding import PartitionSpec as P

MESH = pl.DeviceIdType.MESH
F32, BF16 = jnp.float32, jnp.bfloat16


def split(v):
    hi = v.astype(BF16)
    return hi, (v - hi.astype(F32)).astype(BF16)


def kernel(
    amp, wts, res, out,
    stage, turned, arrived, w_all, w_cross, w_hi, w_lo, l_hi, l_lo, part, relay, final,
    load_sem, wl_sem, w_send, w_recv, own_send, own_recv, give_send, give_recv, core_send, core_recv, z_send, z_recv,
    a_send, a_recv, rel_send, rel_recv, dir_send, dir_recv, mer_send, mer_recv, res_sem,
):
    row, col = lax.axis_index("row"), lax.axis_index("col")
    z, k = row // 2, row % 2
    x, y = col // 4, col % 4
    g = x + k * (y - x)
    s = y + k * (x - y)

    def at(gg, ss):
        return (row, (4 - 3 * k) * (gg % 4) + (1 + 3 * k) * (ss % 4))

    def at_z(zz):
        return (2 * (zz % 4) + k, col)

    other = (2 * z + 1 - k, col)

    def remote(src, dst, send, recv, device):
        return pltpu.make_async_remote_copy(
            src_ref=src, dst_ref=dst, send_sem=send, recv_sem=recv, device_id=device, device_id_type=MESH
        )

    barrier = pltpu.get_barrier_semaphore()
    for d in (1, 2, 3):
        pl.semaphore_signal(barrier, 1, device_id=at(g + d, s), device_id_type=MESH)
    for device in (at(g, s + 1), at(g, s + 3), at_z(z + 1), at_z(z + 3), other):
        pl.semaphore_signal(barrier, 1, device_id=device, device_id_type=MESH)

    half0 = ((s + 2) % 4) // 2

    def block_of(q):
        line0 = 2 * ((g + 1 + 2 * q + (q // 2) % 2) % 4) + (half0 + q // 4) % 2
        m = q // 2
        u = m // 2
        off = (1 - u) * (2 + m) + u * (3 - m)
        line1 = 2 * ((s + off) % 4) + (g // 2 + 1 + q) % 2
        return line0 + k * (line1 - line0)

    def load(q):
        t = block_of(q)
        return pltpu.make_async_copy(
            amp.at[:, :, :, pl.ds(pl.multiple_of(t * 128, 128), 128)], stage.at[q % 2], load_sem.at[q % 2]
        )

    load(0).start()
    load(1).start()
    own_w = pltpu.make_async_copy(wts, w_all.at[row, 0], wl_sem)
    residual = pltpu.make_async_copy(res, out, res_sem)
    own_w.start()

    residual.start()

    pl.semaphore_wait(barrier, 8)

    def w_pass(cross, up, onward):
        step = 1 if up else 3
        device = at(g, s + step) if cross else at(g + step, s)
        rows = pl.ds(0 if up else 2, 2)
        if cross:
            dst = w_cross.at[1, rows] if onward else w_cross.at[2 if up else 0]
            src = w_cross.at[2 if up else 0, rows] if onward else wts
        else:
            dst = w_all.at[row, 2, rows] if onward else w_all.at[row, 3 if up else 1]
            src = w_all.at[row, 3 if up else 1, rows] if onward else wts
        sem = 4 * cross + 2 * onward + (0 if up else 1)
        return remote(src, dst, w_send.at[sem], w_recv.at[sem], device)

    def own_pass(up, onward):
        sem = 2 * onward + (0 if up else 1)
        device = at_z(z + (1 if up else 3))
        if onward:
            rows = pl.ds(0 if up else 2, 2)
            src = w_all.at[2 * ((z + (3 if up else 1)) % 4) + k, 0, rows]
            return remote(src, src, own_send.at[sem], own_recv.at[sem], device)
        return remote(wts, w_all.at[row, 0], own_send.at[sem], own_recv.at[sem], device)

    def give(i):
        if i == 0:
            src, dst = wts, w_all.at[row, 0]
        elif i < 3:
            src = dst = w_all.at[2 * ((z + (3 if i == 1 else 1)) % 4) + k, 0]
        else:
            src = dst = w_all.at[2 * ((z + 2) % 4) + k, 0, pl.ds(0 if i == 3 else 2, 2)]
        return remote(src, dst, give_send.at[i], give_recv.at[i], other)

    for cross in (0, 1):
        w_pass(cross, True, 0).start()
        w_pass(cross, False, 0).start()
    own_pass(True, 0).start()
    own_pass(False, 0).start()
    give(0).start()

    def slab(o):
        xx, yy = o // 4, o % 4
        gg = xx + k * (yy - xx)
        r = yy + k * (xx - yy)
        return gg, r

    def send_slab(o):
        gg, r = slab(o)
        return remote(turned.at[o], arrived.at[r, (g - gg + 4) % 4], a_send.at[o], a_recv.at[4 * r + (g - gg + 4) % 4], at(gg, s))

    def z_copy(n, e, up, sem):
        sl = 2 * (n % 4) + e
        rest = w_all.at[sl, pl.ds(1, 3)]
        return remote(rest, rest, z_send.at[sem], z_recv.at[sem], at_z(z + 1 if up else z + 3))

    def split_w(n):
        n = n % 4

        @pl.loop(0, 4)
        def _(gg):
            for e in range(2):
                hi, lo = split(w_all[2 * n + e, gg].reshape(256, 128))
                at_rows = pl.ds(pl.multiple_of(gg * 256, 256), 256)
                w_hi[n, at_rows, 128 * e : 128 * e + 128] = hi
                w_lo[n, at_rows, 128 * e : 128 * e + 128] = lo

    swap = remote(w_cross, w_all.at[row, pl.ds(1, 3)], core_send, core_recv, other)

    @pl.loop(0, 8)
    def _(q):
        load(q).wait()
        t = block_of(q)
        rows = stage.at[q % 2].reshape(2048, 128)
        for i in range(8):
            v = rows[pl.ds(i, 256, stride=8), :].T
            for e in range(2):
                for h in range(2):
                    turned.at[2 * t + e, h][pl.ds(i, 64, stride=8), :] = v[64 * e : 64 * e + 64, 128 * h : 128 * h + 128]

        @pl.when(q < 6)
        def _():
            load(q + 2).start()

        for e in range(2):
            o = 2 * t + e
            gg, r = slab(o)

            @pl.when((gg != g) & (r != s))
            def _():
                send_slab(o).start()

            @pl.when(gg == g)
            def _():
                pltpu.make_async_copy(turned.at[o], arrived.at[r, 0], a_recv.at[4 * r]).start()

        @pl.when(q == 1)
        def _():
            for cross in (0, 1):
                w_pass(cross, True, 0).wait()
                w_pass(cross, True, 1).start()
                w_pass(cross, False, 0).wait()
                w_pass(cross, False, 1).start()
            own_pass(True, 0).wait()
            own_pass(True, 1).start()
            give(1).start()
            own_pass(False, 0).wait()
            own_pass(False, 1).start()
            give(2).start()

        @pl.when(q == 3)
        def _():
            w_pass(0, True, 1).wait()
            w_pass(0, False, 1).wait()
            z_copy(z, k, True, k).start()
            z_copy(z, k, False, 2 + k).start()
            w_pass(1, True, 1).wait()
            w_pass(1, False, 1).wait()
            swap.start()

        @pl.when(q == 5)
        def _():
            swap.wait()
            z_copy(z, 1 - k, True, 1 - k).start()
            z_copy(z, 1 - k, False, 3 - k).start()
            own_pass(True, 1).wait()
            give(3).start()
            own_pass(False, 1).wait()
            give(4).start()

    for d in (1, 3, 2):
        send_slab(at(g + d, s)[1]).start()

    def a_arrive(r, gg):
        return remote(turned.at[0], arrived.at[r, gg], a_send.at[0], a_recv.at[4 * r + gg], other)

    def piece(j):
        return (z + j + j // 2 - 2 * (j // 3)) % 4

    def weights(j):
        @pl.when(j == 0)
        def _():
            own_w.wait()
            give(0).wait()
            split_w(z)

        @pl.when(j == 1)
        def _():
            z_copy(z, 0, True, 0).wait()
            z_copy(z + 3, 0, True, 4).start()
            z_copy(z, 1, False, 3).wait()
            z_copy(z + 1, 1, False, 5).start()
            z_copy(z, 1, True, 1).wait()
            z_copy(z, 0, False, 2).wait()
            give(1).wait()
            give(2).wait()
            split_w(z + 1)

        @pl.when(j == 2)
        def _():
            split_w(z + 3)

        @pl.when(j == 3)
        def _():
            z_copy(z + 3, 0, True, 4).wait()
            z_copy(z + 1, 1, False, 5).wait()
            give(3).wait()
            give(4).wait()
            split_w(z + 2)

    def multiply(m, r, then):
        r = r % 4
        for gg in range(4):
            a_arrive(r, gg).wait_recv()

        @pl.loop(0, 4)
        def _(gg):
            for h in range(2):
                hi, lo = split(arrived[r, gg, h])
                lanes = pl.ds(pl.multiple_of(256 * gg + 128 * h, 128), 128)
                l_hi[:, lanes] = hi
                l_lo[:, lanes] = lo

        @pl.loop(0, 4)
        def _(j):
            n = piece(j)
            if m == 0:
                weights(j)
            total = jnp.dot(l_hi[...], w_hi[n], preferred_element_type=F32)
            total += jnp.dot(l_hi[...], w_lo[n], preferred_element_type=F32)
            total += jnp.dot(l_lo[...], w_hi[n], preferred_element_type=F32)
            part[m, n] = total.reshape(64, 8, 256)
            if then is not None:
                then(n)

    low, high = pl.ds(0, 32), pl.ds(32, 32)

    def relay_up(n):
        return remote(part.at[0, n, low], relay.at[0, n], rel_send.at[0, n], rel_recv.at[0, n], at(g, s + 1))

    def relay_down(n):
        return remote(part.at[0, n, high], relay.at[1, n], rel_send.at[1, n], rel_recv.at[1, n], at(g, s + 3))

    def direct_up(n):
        return remote(part.at[1, n, high], final.at[0, n, high], dir_send.at[0, n], dir_recv.at[0, n], at(g, s + 1))

    def direct_down(n):
        return remote(part.at[2, n, low], final.at[1, n, low], dir_send.at[1, n], dir_recv.at[1, n], at(g, s + 3))

    def merged_up(n):
        return remote(part.at[1, n, low], final.at[0, n, low], mer_send.at[0, n], mer_recv.at[0, n], at(g, s + 1))

    def merged_down(n):
        return remote(part.at[2, n, high], final.at[1, n, high], mer_send.at[1, n], mer_recv.at[1, n], at(g, s + 3))

    def send_relays(n):
        relay_up(n).start()
        relay_down(n).start()

    multiply(0, s + 2, send_relays)
    multiply(1, s + 1, lambda n: direct_up(n).start())
    multiply(2, s + 3, lambda n: direct_down(n).start())

    @pl.loop(0, 4)
    def _(j):
        n = piece(j)
        relay_up(n).wait()
        part[1, n, low] += relay[0, n]
        merged_up(n).start()
        relay_down(n).wait()
        part[2, n, high] += relay[1, n]
        merged_down(n).start()

    multiply(3, s, None)
    residual.wait()

    @pl.loop(0, 4)
    def _(j):
        n = piece(j)
        direct_up(n).wait()
        direct_down(n).wait()
        merged_up(n).wait()
        merged_down(n).wait()
        out[:, :, pl.ds(pl.multiple_of(n * 256, 256), 256)] += part[3, n] + final[0, n] + final[1, n]

    @pl.loop(0, 16)
    def _(o):
        gg, r = slab(o)

        @pl.when(gg != g)
        def _():
            send_slab(o).wait_send()


def shards(amplitudes, cycle_weights, residual_in):
    dma = pltpu.SemaphoreType.DMA
    return pl.pallas_call(
        kernel,
        out_shape=pltpu.VMEM((64, 8, 1024), F32),
        in_specs=[pl.BlockSpec(memory_space=pl.ANY)] * 3,
        out_specs=pl.BlockSpec(memory_space=pltpu.VMEM),
        scratch_shapes=[
            pltpu.VMEM((2, 4, 64, 8, 128), F32),
            pltpu.VMEM((16, 2, 512, 128), F32),
            pltpu.VMEM((4, 4, 2, 512, 128), F32),
            pltpu.VMEM((8, 4, 4, 64, 128), F32),
            pltpu.VMEM((3, 4, 64, 128), F32),
            pltpu.VMEM((4, 1024, 256), BF16),
            pltpu.VMEM((4, 1024, 256), BF16),
            pltpu.VMEM((512, 1024), BF16),
            pltpu.VMEM((512, 1024), BF16),
            pltpu.VMEM((4, 4, 64, 8, 256), F32),
            pltpu.VMEM((2, 4, 32, 8, 256), F32),
            pltpu.VMEM((2, 4, 64, 8, 256), F32),
            dma((2,)), dma, dma((8,)), dma((8,)), dma((4,)), dma((4,)), dma((5,)), dma((5,)), dma, dma, dma((6,)), dma((6,)),
            dma((16,)), dma((16,)), dma((2, 4)), dma((2, 4)), dma((2, 4)), dma((2, 4)), dma((2, 4)), dma((2, 4)), dma,
        ],
        compiler_params=pltpu.CompilerParams(collective_id=0, has_side_effects=True, vmem_limit_bytes=54 << 20),
        cost_estimate=pl.CostEstimate(flops=2 * 3 * 512 * 4096 * 1024, bytes_accessed=12 << 20, transcendentals=0),
        name="cycle_sum",
    )(amplitudes, cycle_weights, residual_in)


def solution(mesh):
    return jax.shard_map(
        shards,
        mesh=mesh,
        in_specs=(P(None, "col", "row", None), P(None, "col", "row"), P("col", "row", None)),
        out_specs=P("col", "row", None),
        check_vma=False,
    )
```

```python
import jax
import jax.numpy as jnp
from jax import lax
from jax.experimental import pallas as pl
from jax.experimental.pallas import tpu as pltpu
from jax.sharding import PartitionSpec as P

MESH = pl.DeviceIdType.MESH
F32, BF16 = jnp.float32, jnp.bfloat16


def split(v):
    hi = v.astype(BF16)
    return hi, (v - hi.astype(F32)).astype(BF16)


def kernel(
    amp, wts, res, out,
    stage, turned, arrived, w_all, w_cross, w_hi, w_lo, l_hi, l_lo, part, relay, final,
    load_sem, wl_sem, res_sem, w_send, z_send, a_send, p_send,
    w_recv, own_recv, give_recv, core_recv, z_recv, a_recv, rel_recv, dir_recv, mer_recv,
):
    row, col = lax.axis_index("row"), lax.axis_index("col")
    z, k = row // 2, row % 2
    x, y = col // 4, col % 4
    g = x + k * (y - x)
    s = y + k * (x - y)

    def at(gg, ss):
        return (row, (4 - 3 * k) * (gg % 4) + (1 + 3 * k) * (ss % 4))

    def at_z(zz):
        return (2 * (zz % 4) + k, col)

    other = (2 * z + 1 - k, col)

    def remote(src, dst, send, recv, device):
        return pltpu.make_async_remote_copy(
            src_ref=src, dst_ref=dst, send_sem=send, recv_sem=recv, device_id=device, device_id_type=MESH
        )

    def take(ref, sem):
        pltpu.make_async_copy(ref, ref, sem).wait()

    barrier = pltpu.get_barrier_semaphore()
    for d in (1, 2, 3):
        pl.semaphore_signal(barrier, 1, device_id=at(g + d, s), device_id_type=MESH)
    for device in (at(g, s + 1), at(g, s + 3), at_z(z + 1), at_z(z + 3), other):
        pl.semaphore_signal(barrier, 1, device_id=device, device_id_type=MESH)

    half0 = ((s + 2) % 4) // 2

    def block_of(q):
        line0 = 2 * ((g + 1 + 2 * q + (q // 2) % 2) % 4) + (half0 + q // 4) % 2
        m = q // 2
        u = m // 2
        off = (1 - u) * (2 + m) + u * (3 - m)
        line1 = 2 * ((s + off) % 4) + (g // 2 + 1 + q) % 2
        return line0 + k * (line1 - line0)

    def load(q):
        t = block_of(q)
        return pltpu.make_async_copy(
            amp.at[:, :, :, pl.ds(pl.multiple_of(t * 128, 128), 128)], stage.at[q % 2], load_sem.at[q % 2]
        )

    load(0).start()
    load(1).start()
    own_w = pltpu.make_async_copy(wts, w_all.at[row, 0], wl_sem)
    residual = pltpu.make_async_copy(res, out, res_sem)
    own_w.start()

    residual.start()

    pl.semaphore_wait(barrier, 8)

    def w_pass(cross, up, onward):
        step = 1 if up else 3
        device = at(g, s + step) if cross else at(g + step, s)
        rows = pl.ds(0 if up else 2, 2)
        if cross:
            dst = w_cross.at[1, rows] if onward else w_cross.at[2 if up else 0]
            src = w_cross.at[2 if up else 0, rows] if onward else wts
        else:
            dst = w_all.at[row, 2, rows] if onward else w_all.at[row, 3 if up else 1]
            src = w_all.at[row, 3 if up else 1, rows] if onward else wts
        return remote(src, dst, w_send, w_recv.at[1 + cross if onward else 0], device)

    def own_pass(up, onward):
        device = at_z(z + (1 if up else 3))
        if onward:
            rows = pl.ds(0 if up else 2, 2)
            src = w_all.at[2 * ((z + (3 if up else 1)) % 4) + k, 0, rows]
            return remote(src, src, w_send, own_recv.at[1], device)
        return remote(wts, w_all.at[row, 0], w_send, own_recv.at[0], device)

    def give(i):
        if i == 0:
            src, dst = wts, w_all.at[row, 0]
        elif i < 3:
            src = dst = w_all.at[2 * ((z + (3 if i == 1 else 1)) % 4) + k, 0]
        else:
            src = dst = w_all.at[2 * ((z + 2) % 4) + k, 0, pl.ds(0 if i == 3 else 2, 2)]
        return remote(src, dst, w_send, give_recv.at[(i + 1) // 2], other)

    for cross in (0, 1):
        w_pass(cross, True, 0).start()
        w_pass(cross, False, 0).start()
    own_pass(True, 0).start()
    own_pass(False, 0).start()
    give(0).start()

    def slab(o):
        xx, yy = o // 4, o % 4
        gg = xx + k * (yy - xx)
        r = yy + k * (xx - yy)
        return gg, r

    def send_slab(o):
        gg, r = slab(o)
        return remote(turned.at[o], arrived.at[r, (g - gg + 4) % 4], a_send, a_recv.at[r], at(gg, s))

    def z_copy(n, e, up, onward):
        sl = 2 * (n % 4) + e
        rest = w_all.at[sl, pl.ds(1, 3)]
        return remote(rest, rest, z_send, z_recv.at[2 if onward else (e if up else 1 - e)], at_z(z + 1 if up else z + 3))

    def split_w(n):
        n = n % 4

        @pl.loop(0, 4)
        def _(gg):
            for e in range(2):
                hi, lo = split(w_all[2 * n + e, gg].reshape(256, 128))
                at_rows = pl.ds(pl.multiple_of(gg * 256, 256), 256)
                w_hi[n, at_rows, 128 * e : 128 * e + 128] = hi
                w_lo[n, at_rows, 128 * e : 128 * e + 128] = lo

    swap = remote(w_cross, w_all.at[row, pl.ds(1, 3)], w_send, core_recv, other)

    @pl.loop(0, 8)
    def _(q):
        load(q).wait()
        t = block_of(q)
        rows = stage.at[q % 2].reshape(2048, 128)
        for i in range(8):
            v = rows[pl.ds(i, 256, stride=8), :].T
            for e in range(2):
                for h in range(2):
                    turned.at[2 * t + e, h][pl.ds(i, 64, stride=8), :] = v[64 * e : 64 * e + 64, 128 * h : 128 * h + 128]

        @pl.when(q < 6)
        def _():
            load(q + 2).start()

        for e in range(2):
            o = 2 * t + e
            gg, r = slab(o)

            @pl.when((gg != g) & (r != s))
            def _():
                send_slab(o).start()

            @pl.when(gg == g)
            def _():
                pltpu.make_async_copy(turned.at[o], arrived.at[r, 0], a_recv.at[r]).start()

        @pl.when(q == 1)
        def _():
            take(w_all.at[0], w_recv.at[0])
            for cross in (0, 1):
                w_pass(cross, True, 1).start()
                w_pass(cross, False, 1).start()
            take(w_all.at[0, pl.ds(0, 2)], own_recv.at[0])
            own_pass(True, 1).start()
            own_pass(False, 1).start()
            give(1).start()
            give(2).start()

        @pl.when(q == 3)
        def _():
            take(w_all.at[0, 0], w_recv.at[1])
            z_copy(z, k, True, 0).start()
            z_copy(z, k, False, 0).start()
            take(w_all.at[0, 0], w_recv.at[2])
            swap.start()

        @pl.when(q == 5)
        def _():
            take(w_cross, core_recv)
            z_copy(z, 1 - k, True, 0).start()
            z_copy(z, 1 - k, False, 0).start()
            take(w_all.at[0, 0], own_recv.at[1])
            give(3).start()
            give(4).start()

    for d in (1, 3, 2):
        send_slab(at(g + d, s)[1]).start()

    def piece(j):
        return (z + j + j // 2 - 2 * (j // 3)) % 4

    def weights(j):
        @pl.when(j == 0)
        def _():
            own_w.wait()
            take(w_all.at[0, 0], give_recv.at[0])
            split_w(z)

        @pl.when(j == 1)
        def _():
            take(w_all.at[pl.ds(0, 2), pl.ds(1, 3)], z_recv.at[0])
            z_copy(z + 3, 0, True, 1).start()
            z_copy(z + 1, 1, False, 1).start()
            take(w_all.at[pl.ds(0, 2), pl.ds(1, 3)], z_recv.at[1])
            take(w_all.at[0, pl.ds(0, 2)], give_recv.at[1])
            split_w(z + 1)

        @pl.when(j == 2)
        def _():
            split_w(z + 3)

        @pl.when(j == 3)
        def _():
            take(w_all.at[pl.ds(0, 2), pl.ds(1, 3)], z_recv.at[2])
            take(w_all.at[0, 0], give_recv.at[2])
            split_w(z + 2)

    def multiply(m, r, then):
        r = r % 4
        take(arrived.at[r], a_recv.at[r])

        @pl.loop(0, 4)
        def _(gg):
            for h in range(2):
                hi, lo = split(arrived[r, gg, h])
                lanes = pl.ds(pl.multiple_of(256 * gg + 128 * h, 128), 128)
                l_hi[:, lanes] = hi
                l_lo[:, lanes] = lo

        @pl.loop(0, 4)
        def _(j):
            n = piece(j)
            if m == 0:
                weights(j)
            total = jnp.dot(l_hi[...], w_hi[n], preferred_element_type=F32)
            total += jnp.dot(l_hi[...], w_lo[n], preferred_element_type=F32)
            total += jnp.dot(l_lo[...], w_hi[n], preferred_element_type=F32)
            part[m, n] = total.reshape(64, 8, 256)
            if then is not None:
                then(n)

    low, high = pl.ds(0, 32), pl.ds(32, 32)

    def relay_up(n):
        return remote(part.at[0, n, low], relay.at[0, n], p_send, rel_recv.at[n], at(g, s + 1))

    def relay_down(n):
        return remote(part.at[0, n, high], relay.at[1, n], p_send, rel_recv.at[n], at(g, s + 3))

    def direct_up(n):
        return remote(part.at[1, n, high], final.at[0, n, high], p_send, dir_recv, at(g, s + 1))

    def direct_down(n):
        return remote(part.at[2, n, low], final.at[1, n, low], p_send, dir_recv, at(g, s + 3))

    def merged_up(n):
        return remote(part.at[1, n, low], final.at[0, n, low], p_send, mer_recv.at[n], at(g, s + 1))

    def merged_down(n):
        return remote(part.at[2, n, high], final.at[1, n, high], p_send, mer_recv.at[n], at(g, s + 3))

    def send_relays(n):
        relay_up(n).start()
        relay_down(n).start()

    multiply(0, s + 2, send_relays)
    multiply(1, s + 1, lambda n: direct_up(n).start())
    multiply(2, s + 3, lambda n: direct_down(n).start())

    @pl.loop(0, 4)
    def _(j):
        n = piece(j)
        take(relay.at[:, n], rel_recv.at[n])
        part[1, n, low] += relay[0, n]
        merged_up(n).start()
        part[2, n, high] += relay[1, n]
        merged_down(n).start()

    multiply(3, s, None)
    residual.wait()
    take(final.at[0], dir_recv)

    @pl.loop(0, 4)
    def _(j):
        n = piece(j)
        take(final.at[0, n], mer_recv.at[n])
        out[:, :, pl.ds(pl.multiple_of(n * 256, 256), 256)] += part[3, n] + final[0, n] + final[1, n]

    take(w_all.at[pl.ds(0, 4)], w_send)
    take(w_all.at[pl.ds(0, 6), pl.ds(1, 3)], z_send)
    take(turned.at[pl.ds(0, 12)], a_send)
    take(part.at[pl.ds(0, 3)], p_send)


def shards(amplitudes, cycle_weights, residual_in):
    dma = pltpu.SemaphoreType.DMA
    return pl.pallas_call(
        kernel,
        out_shape=pltpu.VMEM((64, 8, 1024), F32),
        in_specs=[pl.BlockSpec(memory_space=pl.ANY)] * 3,
        out_specs=pl.BlockSpec(memory_space=pltpu.VMEM),
        scratch_shapes=[
            pltpu.VMEM((2, 4, 64, 8, 128), F32),
            pltpu.VMEM((16, 2, 512, 128), F32),
            pltpu.VMEM((4, 4, 2, 512, 128), F32),
            pltpu.VMEM((8, 4, 4, 64, 128), F32),
            pltpu.VMEM((3, 4, 64, 128), F32),
            pltpu.VMEM((4, 1024, 256), BF16),
            pltpu.VMEM((4, 1024, 256), BF16),
            pltpu.VMEM((512, 1024), BF16),
            pltpu.VMEM((512, 1024), BF16),
            pltpu.VMEM((4, 4, 64, 8, 256), F32),
            pltpu.VMEM((2, 4, 32, 8, 256), F32),
            pltpu.VMEM((2, 4, 64, 8, 256), F32),
            dma((2,)), dma, dma, dma, dma, dma, dma,
            dma((3,)), dma((2,)), dma((3,)), dma, dma((3,)), dma((4,)), dma((4,)), dma, dma((4,)),
        ],
        compiler_params=pltpu.CompilerParams(collective_id=0, has_side_effects=True, vmem_limit_bytes=54 << 20),
        cost_estimate=pl.CostEstimate(flops=2 * 3 * 512 * 4096 * 1024, bytes_accessed=12 << 20, transcendentals=0),
        name="cycle_sum",
    )(amplitudes, cycle_weights, residual_in)


def solution(mesh):
    return jax.shard_map(
        shards,
        mesh=mesh,
        in_specs=(P(None, "col", "row", None), P(None, "col", "row"), P("col", "row", None)),
        out_specs=P("col", "row", None),
        check_vma=False,
    )
```

```python
import jax
import jax.numpy as jnp
from jax import lax
from jax.experimental import pallas as pl
from jax.experimental.pallas import tpu as pltpu
from jax.sharding import PartitionSpec as P

MESH = pl.DeviceIdType.MESH
F32, BF16 = jnp.float32, jnp.bfloat16


def split(v):
    hi = v.astype(BF16)
    return hi, (v - hi.astype(F32)).astype(BF16)


def kernel(
    amp, wts, res, out,
    stage, turned, arrived, w_all, w_cross, w_hi, w_lo, l_hi, l_lo, part, relay, final,
    load_sem, wl_sem, res_sem, w_send, z_send, a_send, p_send,
    w_recv, own_recv, give_recv, core_recv, z_recv, a_recv, rel_recv, dir_recv, mer_recv,
):
    row, col = lax.axis_index("row"), lax.axis_index("col")
    z, k = row // 2, row % 2
    x, y = col // 4, col % 4
    g = x + k * (y - x)
    s = y + k * (x - y)

    def at(gg, ss):
        return (row, (4 - 3 * k) * (gg % 4) + (1 + 3 * k) * (ss % 4))

    def at_z(zz):
        return (2 * (zz % 4) + k, col)

    other = (2 * z + 1 - k, col)

    def remote(src, dst, send, recv, device):
        return pltpu.make_async_remote_copy(
            src_ref=src, dst_ref=dst, send_sem=send, recv_sem=recv, device_id=device, device_id_type=MESH
        )

    def take(ref, sem):
        pltpu.make_async_copy(ref, ref, sem).wait()

    barrier = pltpu.get_barrier_semaphore()
    for d in (1, 2, 3):
        pl.semaphore_signal(barrier, 1, device_id=at(g + d, s), device_id_type=MESH)
    for device in (at(g, s + 1), at(g, s + 3), at_z(z + 1), at_z(z + 3), other):
        pl.semaphore_signal(barrier, 1, device_id=device, device_id_type=MESH)

    half0 = ((s + 2) % 4) // 2

    def block_of(q):
        line0 = 2 * ((g + 1 + 2 * q + (q // 2) % 2) % 4) + (half0 + q // 4) % 2
        m = q // 2
        u = m // 2
        off = (1 - u) * (2 + m) + u * (3 - m)
        line1 = 2 * ((s + off) % 4) + (g // 2 + q) % 2
        return line0 + k * (line1 - line0)

    def load(q):
        t = block_of(q)
        return pltpu.make_async_copy(
            amp.at[:, :, :, pl.ds(pl.multiple_of(t * 128, 128), 128)], stage.at[q % 2], load_sem.at[q % 2]
        )

    load(0).start()
    load(1).start()
    own_w = pltpu.make_async_copy(wts, w_all.at[row, 0], wl_sem)
    residual = pltpu.make_async_copy(res, out, res_sem)
    own_w.start()

    residual.start()

    pl.semaphore_wait(barrier, 8)

    def w_pass(cross, up, onward):
        step = 1 if up else 3
        device = at(g, s + step) if cross else at(g + step, s)
        rows = pl.ds(0 if up else 2, 2)
        if cross:
            dst = w_cross.at[1, rows] if onward else w_cross.at[2 if up else 0]
            src = w_cross.at[2 if up else 0, rows] if onward else wts
        else:
            dst = w_all.at[row, 2, rows] if onward else w_all.at[row, 3 if up else 1]
            src = w_all.at[row, 3 if up else 1, rows] if onward else wts
        return remote(src, dst, w_send, w_recv.at[1 + cross if onward else 0], device)

    def own_pass(up, onward):
        device = at_z(z + (1 if up else 3))
        if onward:
            rows = pl.ds(0 if up else 2, 2)
            src = w_all.at[2 * ((z + (3 if up else 1)) % 4) + k, 0, rows]
            return remote(src, src, w_send, own_recv.at[1], device)
        return remote(wts, w_all.at[row, 0], w_send, own_recv.at[0], device)

    def give(i):
        if i == 0:
            src, dst = wts, w_all.at[row, 0]
        elif i < 3:
            src = dst = w_all.at[2 * ((z + (3 if i == 1 else 1)) % 4) + k, 0]
        else:
            src = dst = w_all.at[2 * ((z + 2) % 4) + k, 0, pl.ds(0 if i == 3 else 2, 2)]
        return remote(src, dst, w_send, give_recv.at[(i + 1) // 2], other)

    for cross in (0, 1):
        w_pass(cross, True, 0).start()
        w_pass(cross, False, 0).start()
    own_pass(True, 0).start()
    own_pass(False, 0).start()
    give(0).start()

    def slab(o):
        xx, yy = o // 4, o % 4
        gg = xx + k * (yy - xx)
        r = yy + k * (xx - yy)
        return gg, r

    def send_slab(o):
        gg, r = slab(o)
        return remote(turned.at[o], arrived.at[r, (g - gg + 4) % 4], a_send, a_recv.at[r], at(gg, s))

    def z_copy(n, e, up, onward):
        sl = 2 * (n % 4) + e
        rest = w_all.at[sl, pl.ds(1, 3)]
        return remote(rest, rest, z_send, z_recv.at[2 if onward else (e if up else 1 - e)], at_z(z + 1 if up else z + 3))

    def split_w(n):
        n = n % 4

        @pl.loop(0, 4)
        def _(gg):
            for e in range(2):
                hi, lo = split(w_all[2 * n + e, gg].reshape(256, 128))
                at_rows = pl.ds(pl.multiple_of(gg * 256, 256), 256)
                w_hi[n, at_rows, 128 * e : 128 * e + 128] = hi
                w_lo[n, at_rows, 128 * e : 128 * e + 128] = lo

    swap = remote(w_cross, w_all.at[row, pl.ds(1, 3)], w_send, core_recv, other)

    @pl.loop(0, 8)
    def _(q):
        load(q).wait()
        t = block_of(q)
        rows = stage.at[q % 2].reshape(2048, 128)
        for i in range(8):
            v = rows[pl.ds(i, 256, stride=8), :].T
            for e in range(2):
                for h in range(2):
                    turned.at[2 * t + e, h][pl.ds(i, 64, stride=8), :] = v[64 * e : 64 * e + 64, 128 * h : 128 * h + 128]

        @pl.when(q < 6)
        def _():
            load(q + 2).start()

        for e in range(2):
            o = 2 * t + e
            gg, r = slab(o)

            @pl.when((gg != g) & (r != s))
            def _():
                send_slab(o).start()

            @pl.when(gg == g)
            def _():
                pltpu.make_async_copy(turned.at[o], arrived.at[r, 0], a_recv.at[r]).start()

        @pl.when(q == 1)
        def _():
            take(w_all.at[0], w_recv.at[0])
            for cross in (0, 1):
                w_pass(cross, True, 1).start()
                w_pass(cross, False, 1).start()
            take(w_all.at[0, pl.ds(0, 2)], own_recv.at[0])
            own_pass(True, 1).start()
            own_pass(False, 1).start()
            give(1).start()
            give(2).start()

        @pl.when(q == 3)
        def _():
            take(w_all.at[0, 0], w_recv.at[1])
            z_copy(z, k, True, 0).start()
            z_copy(z, k, False, 0).start()
            take(w_all.at[0, 0], w_recv.at[2])
            swap.start()

        @pl.when(q == 5)
        def _():
            take(w_cross, core_recv)
            z_copy(z, 1 - k, True, 0).start()
            z_copy(z, 1 - k, False, 0).start()
            take(w_all.at[0, 0], own_recv.at[1])
            give(3).start()
            give(4).start()

    for d in (1, 3, 2):
        send_slab(at(g + d, s)[1]).start()

    def piece(j):
        return (z + j + j // 2 - 2 * (j // 3)) % 4

    def weights(j):
        @pl.when(j == 0)
        def _():
            own_w.wait()
            take(w_all.at[0, 0], give_recv.at[0])
            split_w(z)

        @pl.when(j == 1)
        def _():
            take(w_all.at[pl.ds(0, 2), pl.ds(1, 3)], z_recv.at[0])
            z_copy(z + 3, 0, True, 1).start()
            z_copy(z + 1, 1, False, 1).start()
            take(w_all.at[pl.ds(0, 2), pl.ds(1, 3)], z_recv.at[1])
            take(w_all.at[0, pl.ds(0, 2)], give_recv.at[1])
            split_w(z + 1)

        @pl.when(j == 2)
        def _():
            split_w(z + 3)

        @pl.when(j == 3)
        def _():
            take(w_all.at[pl.ds(0, 2), pl.ds(1, 3)], z_recv.at[2])
            take(w_all.at[0, 0], give_recv.at[2])
            split_w(z + 2)

    def multiply(m, r, then):
        r = r % 4
        take(arrived.at[r], a_recv.at[r])

        @pl.loop(0, 4)
        def _(gg):
            for h in range(2):
                hi, lo = split(arrived[r, gg, h])
                lanes = pl.ds(pl.multiple_of(256 * gg + 128 * h, 128), 128)
                l_hi[:, lanes] = hi
                l_lo[:, lanes] = lo

        @pl.loop(0, 4)
        def _(j):
            n = piece(j)
            if m == 0:
                weights(j)
            total = jnp.dot(l_hi[...], w_hi[n], preferred_element_type=F32)
            total += jnp.dot(l_hi[...], w_lo[n], preferred_element_type=F32)
            total += jnp.dot(l_lo[...], w_hi[n], preferred_element_type=F32)
            part[m, n] = total.reshape(64, 8, 256)
            if then is not None:
                then(n)

    low, high = pl.ds(0, 32), pl.ds(32, 32)

    def relay_up(n):
        return remote(part.at[0, n, low], relay.at[0, n], p_send, rel_recv.at[n], at(g, s + 1))

    def relay_down(n):
        return remote(part.at[0, n, high], relay.at[1, n], p_send, rel_recv.at[n], at(g, s + 3))

    def direct_up(n):
        return remote(part.at[1, n, high], final.at[0, n, high], p_send, dir_recv, at(g, s + 1))

    def direct_down(n):
        return remote(part.at[2, n, low], final.at[1, n, low], p_send, dir_recv, at(g, s + 3))

    def merged_up(n):
        return remote(part.at[1, n, low], final.at[0, n, low], p_send, mer_recv.at[n], at(g, s + 1))

    def merged_down(n):
        return remote(part.at[2, n, high], final.at[1, n, high], p_send, mer_recv.at[n], at(g, s + 3))

    def send_relays(n):
        relay_up(n).start()
        relay_down(n).start()

    multiply(0, s + 2, send_relays)
    multiply(1, s + 1, lambda n: direct_up(n).start())
    multiply(2, s + 3, lambda n: direct_down(n).start())

    @pl.loop(0, 4)
    def _(j):
        n = piece(j)
        take(relay.at[:, n], rel_recv.at[n])
        part[1, n, low] += relay[0, n]
        merged_up(n).start()
        part[2, n, high] += relay[1, n]
        merged_down(n).start()

    multiply(3, s, None)
    residual.wait()
    take(final.at[0], dir_recv)

    def lanes(n):
        return pl.ds(pl.multiple_of(n * 256, 256), 256)

    @pl.loop(0, 4)
    def _(n):
        out[:32, :, lanes(n)] += part[3, n, low] + final[1, n, low]
        out[32:, :, lanes(n)] += part[3, n, high] + final[0, n, high]

    @pl.loop(0, 4)
    def _(j):
        n = piece(j)
        take(final.at[0, n], mer_recv.at[n])
        out[:32, :, lanes(n)] += final[0, n, low]
        out[32:, :, lanes(n)] += final[1, n, high]

    take(w_all.at[pl.ds(0, 4)], w_send)
    take(w_all.at[pl.ds(0, 6), pl.ds(1, 3)], z_send)
    take(turned.at[pl.ds(0, 12)], a_send)
    take(part.at[pl.ds(0, 3)], p_send)


def shards(amplitudes, cycle_weights, residual_in):
    dma = pltpu.SemaphoreType.DMA
    return pl.pallas_call(
        kernel,
        out_shape=pltpu.VMEM((64, 8, 1024), F32),
        in_specs=[pl.BlockSpec(memory_space=pl.ANY)] * 3,
        out_specs=pl.BlockSpec(memory_space=pltpu.VMEM),
        scratch_shapes=[
            pltpu.VMEM((2, 4, 64, 8, 128), F32),
            pltpu.VMEM((16, 2, 512, 128), F32),
            pltpu.VMEM((4, 4, 2, 512, 128), F32),
            pltpu.VMEM((8, 4, 4, 64, 128), F32),
            pltpu.VMEM((3, 4, 64, 128), F32),
            pltpu.VMEM((4, 1024, 256), BF16),
            pltpu.VMEM((4, 1024, 256), BF16),
            pltpu.VMEM((512, 1024), BF16),
            pltpu.VMEM((512, 1024), BF16),
            pltpu.VMEM((4, 4, 64, 8, 256), F32),
            pltpu.VMEM((2, 4, 32, 8, 256), F32),
            pltpu.VMEM((2, 4, 64, 8, 256), F32),
            dma((2,)), dma, dma, dma, dma, dma, dma,
            dma((3,)), dma((2,)), dma((3,)), dma, dma((3,)), dma((4,)), dma((4,)), dma, dma((4,)),
        ],
        compiler_params=pltpu.CompilerParams(collective_id=0, has_side_effects=True, vmem_limit_bytes=54 << 20),
        cost_estimate=pl.CostEstimate(flops=2 * 3 * 512 * 4096 * 1024, bytes_accessed=12 << 20, transcendentals=0),
        name="cycle_sum",
    )(amplitudes, cycle_weights, residual_in)


def solution(mesh):
    return jax.shard_map(
        shards,
        mesh=mesh,
        in_specs=(P(None, "col", "row", None), P(None, "col", "row"), P("col", "row", None)),
        out_specs=P("col", "row", None),
        check_vma=False,
    )
```

```python
import jax
import jax.numpy as jnp
from jax import lax
from jax.experimental import pallas as pl
from jax.experimental.pallas import tpu as pltpu
from jax.sharding import PartitionSpec as P

MESH = pl.DeviceIdType.MESH
F32, BF16 = jnp.float32, jnp.bfloat16


def split(v):
    hi = v.astype(BF16)
    return hi, (v - hi.astype(F32)).astype(BF16)


def kernel(
    amp, wts, res, out,
    stage, turned, arrived, w_all, w_cross, w_hi, w_lo, l_hi, l_lo, part, relay, final,
    load_sem, wl_sem, res_sem, w_send, z_send, a_send, p_send,
    w_recv, own_recv, give_recv, core_recv, z_recv, a_recv, rel_recv, dir_recv, mer_recv,
):
    row, col = lax.axis_index("row"), lax.axis_index("col")
    z, k = row // 2, row % 2
    x, y = col // 4, col % 4
    g = x + k * (y - x)
    s = y + k * (x - y)

    def at(gg, ss):
        return (row, (4 - 3 * k) * (gg % 4) + (1 + 3 * k) * (ss % 4))

    def at_z(zz):
        return (2 * (zz % 4) + k, col)

    other = (2 * z + 1 - k, col)

    def remote(src, dst, send, recv, device):
        return pltpu.make_async_remote_copy(
            src_ref=src, dst_ref=dst, send_sem=send, recv_sem=recv, device_id=device, device_id_type=MESH
        )

    def take(ref, sem):
        pltpu.make_async_copy(ref, ref, sem).wait()

    barrier = pltpu.get_barrier_semaphore()
    for d in (1, 2, 3):
        pl.semaphore_signal(barrier, 1, device_id=at(g + d, s), device_id_type=MESH)
    for device in (at(g, s + 1), at(g, s + 3), at_z(z + 1), at_z(z + 3), other):
        pl.semaphore_signal(barrier, 1, device_id=device, device_id_type=MESH)

    half0 = ((s + 2) % 4) // 2

    def block_of(q):
        line0 = 2 * ((g + 1 + 2 * q + (q // 2) % 2) % 4) + (half0 + q // 4) % 2
        m = q // 2
        u = m // 2
        off = (1 - u) * (2 + m) + u * (3 - m)
        line1 = 2 * ((s + off) % 4) + (g // 2 + q) % 2
        return line0 + k * (line1 - line0)

    def load(q):
        t = block_of(q)
        return pltpu.make_async_copy(
            amp.at[:, :, :, pl.ds(pl.multiple_of(t * 128, 128), 128)], stage.at[q % 2], load_sem.at[q % 2]
        )

    load(0).start()
    load(1).start()
    own_w = pltpu.make_async_copy(wts, w_all.at[row, 0], wl_sem)
    residual = pltpu.make_async_copy(res, out, res_sem)
    own_w.start()

    residual.start()

    pl.semaphore_wait(barrier, 8)

    def w_pass(cross, up, onward):
        step = 1 if up else 3
        device = at(g, s + step) if cross else at(g + step, s)
        rows = pl.ds(0 if up else 2, 2)
        if cross:
            dst = w_cross.at[1, rows] if onward else w_cross.at[2 if up else 0]
            src = w_cross.at[2 if up else 0, rows] if onward else wts
        else:
            dst = w_all.at[row, 2, rows] if onward else w_all.at[row, 3 if up else 1]
            src = w_all.at[row, 3 if up else 1, rows] if onward else wts
        return remote(src, dst, w_send, w_recv.at[1 + cross if onward else 0], device)

    def own_pass(up, onward):
        device = at_z(z + (1 if up else 3))
        if onward:
            rows = pl.ds(0 if up else 2, 2)
            src = w_all.at[2 * ((z + (3 if up else 1)) % 4) + k, 0, rows]
            return remote(src, src, w_send, own_recv.at[1], device)
        return remote(wts, w_all.at[row, 0], w_send, own_recv.at[0], device)

    def give(i):
        if i == 0:
            src, dst = wts, w_all.at[row, 0]
        elif i < 3:
            src = dst = w_all.at[2 * ((z + (3 if i == 1 else 1)) % 4) + k, 0]
        else:
            src = dst = w_all.at[2 * ((z + 2) % 4) + k, 0, pl.ds(0 if i == 3 else 2, 2)]
        return remote(src, dst, w_send, give_recv.at[(i + 1) // 2], other)

    for cross in (0, 1):
        w_pass(cross, True, 0).start()
        w_pass(cross, False, 0).start()
    own_pass(True, 0).start()
    own_pass(False, 0).start()
    give(0).start()

    def slab(o):
        xx, yy = o // 4, o % 4
        gg = xx + k * (yy - xx)
        r = yy + k * (xx - yy)
        return gg, r

    def send_slab(o):
        gg, r = slab(o)
        return remote(turned.at[o], arrived.at[r, (g - gg + 4) % 4], a_send, a_recv.at[r], at(gg, s))

    def z_copy(n, e, up, onward):
        sl = 2 * (n % 4) + e
        rest = w_all.at[sl, pl.ds(1, 3)]
        return remote(rest, rest, z_send, z_recv.at[2 if onward else (e if up else 1 - e)], at_z(z + 1 if up else z + 3))

    def split_w(n):
        n = n % 4

        @pl.loop(0, 4)
        def _(gg):
            for e in range(2):
                hi, lo = split(w_all[2 * n + e, gg].reshape(256, 128))
                at_rows = pl.ds(pl.multiple_of(gg * 256, 256), 256)
                w_hi[n, at_rows, 128 * e : 128 * e + 128] = hi
                w_lo[n, at_rows, 128 * e : 128 * e + 128] = lo

    swap = remote(w_cross, w_all.at[row, pl.ds(1, 3)], w_send, core_recv, other)

    @pl.loop(0, 8)
    def _(q):
        load(q).wait()
        t = block_of(q)
        rows = stage.at[q % 2].reshape(2048, 128)
        for i in range(8):
            v = rows[pl.ds(i, 256, stride=8), :].T
            for e in range(2):
                for h in range(2):
                    turned.at[2 * t + e, h][pl.ds(i, 64, stride=8), :] = v[64 * e : 64 * e + 64, 128 * h : 128 * h + 128]

        @pl.when(q < 6)
        def _():
            load(q + 2).start()

        for e in range(2):
            o = 2 * t + e
            gg, r = slab(o)

            @pl.when((gg != g) & (r != s))
            def _():
                send_slab(o).start()

            @pl.when(gg == g)
            def _():
                pltpu.make_async_copy(turned.at[o], arrived.at[r, 0], a_recv.at[r]).start()

        @pl.when(q == 1)
        def _():
            take(w_all.at[0], w_recv.at[0])
            for cross in (0, 1):
                w_pass(cross, True, 1).start()
                w_pass(cross, False, 1).start()
            take(w_all.at[0, pl.ds(0, 2)], own_recv.at[0])
            own_pass(True, 1).start()
            own_pass(False, 1).start()
            give(1).start()
            give(2).start()

        @pl.when(q == 3)
        def _():
            take(w_all.at[0, 0], w_recv.at[1])
            z_copy(z, k, True, 0).start()
            z_copy(z, k, False, 0).start()
            take(w_all.at[0, 0], w_recv.at[2])
            swap.start()

        @pl.when(q == 5)
        def _():
            take(w_cross, core_recv)
            z_copy(z, 1 - k, True, 0).start()
            z_copy(z, 1 - k, False, 0).start()
            take(w_all.at[0, 0], own_recv.at[1])
            give(3).start()
            give(4).start()

    for d in (1, 3, 2):
        send_slab(at(g + d, s)[1]).start()

    def piece(j):
        return (z + j + j // 2 - 2 * (j // 3)) % 4

    def weights(j):
        @pl.when(j == 0)
        def _():
            own_w.wait()
            take(w_all.at[0, 0], give_recv.at[0])
            split_w(z)

        @pl.when(j == 1)
        def _():
            take(w_all.at[pl.ds(0, 2), pl.ds(1, 3)], z_recv.at[0])
            z_copy(z + 3, 0, True, 1).start()
            z_copy(z + 1, 1, False, 1).start()
            take(w_all.at[pl.ds(0, 2), pl.ds(1, 3)], z_recv.at[1])
            take(w_all.at[0, pl.ds(0, 2)], give_recv.at[1])
            split_w(z + 1)

        @pl.when(j == 2)
        def _():
            split_w(z + 3)

        @pl.when(j == 3)
        def _():
            take(w_all.at[pl.ds(0, 2), pl.ds(1, 3)], z_recv.at[2])
            take(w_all.at[0, 0], give_recv.at[2])
            split_w(z + 2)

    def multiply(m, r, then):
        r = r % 4
        take(arrived.at[r], a_recv.at[r])

        @pl.loop(0, 4)
        def _(gg):
            for h in range(2):
                hi, lo = split(arrived[r, gg, h])
                lanes = pl.ds(pl.multiple_of(256 * gg + 128 * h, 128), 128)
                l_hi[:, lanes] = hi
                l_lo[:, lanes] = lo

        @pl.loop(0, 4)
        def _(j):
            n = piece(j)
            if m == 0:
                weights(j)
            total = jnp.dot(l_hi[...], w_hi[n], preferred_element_type=F32)
            total += jnp.dot(l_hi[...], w_lo[n], preferred_element_type=F32)
            total += jnp.dot(l_lo[...], w_hi[n], preferred_element_type=F32)
            part[m, n] = total.reshape(64, 8, 256)
            if then is not None:
                then(n)

    low, high = pl.ds(0, 32), pl.ds(32, 32)

    def relay_up(n):
        return remote(part.at[0, n, low], relay.at[0, n], p_send, rel_recv.at[0, n], at(g, s + 1))

    def relay_down(n):
        return remote(part.at[0, n, high], relay.at[1, n], p_send, rel_recv.at[1, n], at(g, s + 3))

    def direct_up(n):
        return remote(part.at[1, n, high], final.at[0, n, high], p_send, dir_recv, at(g, s + 1))

    def direct_down(n):
        return remote(part.at[2, n, low], final.at[1, n, low], p_send, dir_recv, at(g, s + 3))

    def merged_up(n):
        return remote(part.at[1, n, low], final.at[0, n, low], p_send, mer_recv.at[n], at(g, s + 1))

    def merged_down(n):
        return remote(part.at[2, n, high], final.at[1, n, high], p_send, mer_recv.at[n], at(g, s + 3))

    def send_relays(n):
        relay_up(n).start()
        relay_down(n).start()

    multiply(0, s + 2, send_relays)
    multiply(1, s + 1, lambda n: direct_up(n).start())
    multiply(2, s + 3, lambda n: direct_down(n).start())

    @pl.loop(0, 4)
    def _(j):
        n = piece(j)
        take(relay.at[0, n], rel_recv.at[0, n])
        part[1, n, low] += relay[0, n]
        merged_up(n).start()
        take(relay.at[1, n], rel_recv.at[1, n])
        part[2, n, high] += relay[1, n]
        merged_down(n).start()

    multiply(3, s, None)
    residual.wait()
    take(final.at[0], dir_recv)

    def lanes(n):
        return pl.ds(pl.multiple_of(n * 256, 256), 256)

    @pl.loop(0, 4)
    def _(n):
        out[:32, :, lanes(n)] += part[3, n, low] + final[1, n, low]
        out[32:, :, lanes(n)] += part[3, n, high] + final[0, n, high]

    @pl.loop(0, 4)
    def _(j):
        n = piece(j)
        take(final.at[0, n], mer_recv.at[n])
        out[:32, :, lanes(n)] += final[0, n, low]
        out[32:, :, lanes(n)] += final[1, n, high]

    take(w_all.at[pl.ds(0, 4)], w_send)
    take(w_all.at[pl.ds(0, 6), pl.ds(1, 3)], z_send)
    take(turned.at[pl.ds(0, 12)], a_send)
    take(part.at[pl.ds(0, 3)], p_send)


def shards(amplitudes, cycle_weights, residual_in):
    dma = pltpu.SemaphoreType.DMA
    return pl.pallas_call(
        kernel,
        out_shape=pltpu.VMEM((64, 8, 1024), F32),
        in_specs=[pl.BlockSpec(memory_space=pl.ANY)] * 3,
        out_specs=pl.BlockSpec(memory_space=pltpu.VMEM),
        scratch_shapes=[
            pltpu.VMEM((2, 4, 64, 8, 128), F32),
            pltpu.VMEM((16, 2, 512, 128), F32),
            pltpu.VMEM((4, 4, 2, 512, 128), F32),
            pltpu.VMEM((8, 4, 4, 64, 128), F32),
            pltpu.VMEM((3, 4, 64, 128), F32),
            pltpu.VMEM((4, 1024, 256), BF16),
            pltpu.VMEM((4, 1024, 256), BF16),
            pltpu.VMEM((512, 1024), BF16),
            pltpu.VMEM((512, 1024), BF16),
            pltpu.VMEM((4, 4, 64, 8, 256), F32),
            pltpu.VMEM((2, 4, 32, 8, 256), F32),
            pltpu.VMEM((2, 4, 64, 8, 256), F32),
            dma((2,)), dma, dma, dma, dma, dma, dma,
            dma((3,)), dma((2,)), dma((3,)), dma, dma((3,)), dma((4,)), dma((2, 4)), dma, dma((4,)),
        ],
        compiler_params=pltpu.CompilerParams(collective_id=0, has_side_effects=True, vmem_limit_bytes=54 << 20),
        cost_estimate=pl.CostEstimate(flops=2 * 3 * 512 * 4096 * 1024, bytes_accessed=12 << 20, transcendentals=0),
        name="cycle_sum",
    )(amplitudes, cycle_weights, residual_in)


def solution(mesh):
    return jax.shard_map(
        shards,
        mesh=mesh,
        in_specs=(P(None, "col", "row", None), P(None, "col", "row"), P("col", "row", None)),
        out_specs=P("col", "row", None),
        check_vma=False,
    )
```
